256 devices in a mesh: inp: 128 (over x, y, z), tm: 2 (over core).
Axes of the slice: x: 4, y: 4, z: 8, core: 2. Of those that a mesh axis runs over, the one named last changes fastest.
Arguments:
- samples: bfloat16 [512, 2, 131, 2048], P('inp', 'tm'), may hold values from -6 to 6
- pfb_weights: float32 [4, 2048], replicated, may hold values from -3 to 3
Outputs:
- visibility: float32 [1024, 512, 512], P(('inp', 'tm'))
The draws below stay inside these ranges and needn't reach their ends.
All inputs are finite; a program needn't handle non-finite values.
Results may differ from the reference program's by a relative error of at most 0.0046.
Values may be sent and summed in bfloat16 or wider, within the bound.
A program may use at most 128 MiB of HBM per device.

```python
import math
import jax
import jax.numpy as jnp
from jax import lax

INPUTS = 512
CH = 1024
NFFT = 2048
TAPS = 4
S_DEV = 128
BLOCKS = 2
SPECTRA = 256


def block_scale(key, dims, cuts, smallest, high):
    loudness = 1.0
    for position, shards_of in cuts:
        draws = jax.random.uniform(jax.random.fold_in(jax.random.fold_in(key, 6), position), (shards_of,), jnp.float32, smallest / len(cuts), high / len(cuts))
        loudness = loudness * jnp.repeat(jnp.exp(draws), dims[position] // shards_of).reshape((-1,) + (1,) * (len(dims) - 1 - position))
    return loudness


def gaussian(rng, extent, scale, bound, shards=(), kind=jnp.bfloat16):
    entries = scale * jax.random.normal(rng, extent, jnp.float32)
    if shards:
        entries = entries * block_scale(rng, extent, shards, -0.22, 0.18)
    return jnp.clip(entries, -bound, bound).astype(kind)


def setup_inputs(seed: int = 0) -> dict:
    splits = jax.random.split(jax.random.key(seed), 3)
    return {
        "samples": gaussian(splits[0], (INPUTS, BLOCKS, S_DEV + TAPS - 1, NFFT), 1.0, 6.0, ((0, 128), (1, 2))),
        "pfb_weights": gaussian(splits[1], (TAPS, NFFT), 0.5, 3.0, (), jnp.float32),
    }


def dft_table(channels, length):
    index_n = jnp.arange(length, dtype=jnp.int32)
    index_k = jnp.arange(channels, dtype=jnp.int32)
    phase = index_k[:, None] * index_n[None, :] % length
    angle = phase.astype(jnp.float32) * (2.0 * math.pi / length)
    return jnp.stack([jnp.cos(angle), -jnp.sin(angle)]).astype(jnp.bfloat16)

def reference(samples, pfb_weights):
    table = dft_table(CH, NFFT).astype(jnp.float32)
    scale = math.sqrt(2.0 / NFFT)
    groups = samples.reshape(INPUTS // 8, 8, BLOCKS, S_DEV + TAPS - 1, NFFT)

    def channelize(group):
        total = jnp.zeros((8, BLOCKS, S_DEV, NFFT), jnp.float32)
        for tap in range(TAPS):
            total = total + pfb_weights[tap] * group[:, :, tap:tap + S_DEV].astype(jnp.float32)
        filtered = total.astype(jnp.bfloat16).reshape(8, SPECTRA, NFFT).astype(jnp.float32)
        spectra = jnp.einsum('rkn,asn->kras', table, filtered)
        return (spectra * scale).astype(jnp.bfloat16)
    parts = lax.map(channelize, groups)
    spectra = jnp.transpose(parts, (1, 2, 0, 3, 4)).reshape(CH, 2 * INPUTS, SPECTRA)
    rows = jnp.arange(INPUTS, dtype=jnp.int32)
    lower = rows[:, None] >= rows[None, :]

    def correlate(stacked):
        gram = jnp.dot(stacked, stacked.T, preferred_element_type=jnp.float32)
        real_part = gram[:INPUTS, :INPUTS] + gram[INPUTS:, INPUTS:]
        imag_part = gram[INPUTS:, :INPUTS] - gram[:INPUTS, INPUTS:]
        return jnp.where(lower, real_part, imag_part) / SPECTRA
    return lax.map(correlate, spectra)
```

```python
import functools
import math

import jax
import jax.numpy as jnp
import ml_dtypes
import numpy as np
from jax import lax
from jax.experimental import pallas as pl
from jax.experimental.pallas import tpu as pltpu
from jax.sharding import PartitionSpec as P

MESH = pl.DeviceIdType.MESH
VMEM_LIMIT = 48 * 1024 * 1024
LAYERS = 8
CORES = 2


def dft_table(channels, length, scale):
    phase = np.arange(channels)[:, None] * np.arange(length)[None, :] % length
    angle = np.arange(length) * (2.0 * math.pi / length)
    rows = np.stack([np.cos(angle)[phase], -np.sin(angle)[phase]], axis=1) * scale
    return rows.reshape(channels * 2, length).astype(ml_dtypes.bfloat16)


def turn_kernel(
    samples, weights, table, turned, frames, filtered, coeffs, outbox, inbox, table_sem, send_sem, recv_sem
):
    position, core = lax.axis_index("inp"), lax.axis_index("tm")
    group, layer = position // LAYERS, position % LAYERS
    me = position * CORES + core
    groups, rows, length = coeffs.shape
    devices = groups * LAYERS * CORES
    inputs, _, _ = samples.shape
    spectra = filtered.shape[0] // inputs
    taps = weights.shape[0]
    peers = LAYERS * CORES

    def fetch(step):
        chunk = lax.rem(group + step, groups)
        return pltpu.make_async_copy(table.at[chunk], coeffs.at[step], table_sem.at[step])

    def start_fetch(step, carry):
        fetch(step).start()
        return carry

    lax.fori_loop(0, groups, start_fetch, 0)

    barrier = pltpu.get_barrier_semaphore()

    def greet(step, carry):
        other = lax.rem(me + step, devices)
        pl.semaphore_signal(
            barrier, inc=1, device_id=(other // CORES, lax.rem(other, CORES)), device_id_type=MESH
        )
        return carry

    lax.fori_loop(1, devices, greet, 0)

    for a in range(inputs):
        def columns(j, carry):
            cols = pl.ds(pl.multiple_of(j * 128, 128), 128)
            frames[...] = samples[a, :, cols].astype(jnp.float32)
            total = weights[0:1, cols] * frames[0:spectra]
            for tap in range(1, taps):
                total = total + weights[tap : tap + 1, cols] * frames[tap : tap + spectra]
            filtered[a * spectra : (a + 1) * spectra, cols] = total.astype(jnp.bfloat16)
            return carry

        lax.fori_loop(0, length // 128, columns, 0)

    pl.semaphore_wait(barrier, devices - 1)

    half = filtered.shape[0] // 2

    def send_group(step, carry):
        fetch(step).wait()
        found = lax.dot_general(
            coeffs[step], filtered[...], (((1,), (1,)), ((), ())), preferred_element_type=jnp.float32
        )
        found = found.reshape(peers, rows // peers, 2 * half)
        message = jnp.concatenate([found[:, :, :half], found[:, :, half:]], axis=1)
        outbox[pl.ds(step * peers, peers)] = message.astype(jnp.bfloat16)
        to_group = lax.rem(group + step, groups)
        for turn in (4, 3, 5, 2, 6, 1, 7, 0):
            for flip in (0, 1):
                to_layer = lax.rem(layer + turn, LAYERS)
                to_core = lax.rem(core + flip, CORES)
                source = outbox.at[step * peers + to_layer * CORES + to_core]

                def remote():
                    pltpu.make_async_remote_copy(
                        src_ref=source,
                        dst_ref=inbox.at[core, position],
                        send_sem=send_sem,
                        recv_sem=recv_sem.at[group],
                        device_id=(to_group * LAYERS + to_layer, to_core),
                        device_id_type=MESH,
                    ).start()

                if turn == 0 and flip == 0:
                    pl.when(step > 0)(remote)

                    @pl.when(step == 0)
                    def _():
                        pltpu.make_async_copy(source, inbox.at[core, position], recv_sem.at[group]).start()
                else:
                    remote()
        return carry

    lax.fori_loop(0, groups, send_group, 0)

    size = rows * 2
    out_row = lax.broadcasted_iota(jnp.int32, (size, size), 0)
    in_row = lax.broadcasted_iota(jnp.int32, (size, size), 1)
    wanted = (
        (out_row % 2) * (size // 2)
        + (out_row // 4 % LAYERS) * 16
        + (out_row // 2 % 2) * 8
        + (out_row // 64) * 2
        + (out_row // 32 % 2)
    )
    permute = jnp.where(in_row == wanted, 1.0, 0.0).astype(jnp.bfloat16)

    def receive_group(step, carry):
        from_group = lax.rem(group + groups - step, groups)
        landed = inbox.at[:, pl.ds(from_group * LAYERS, LAYERS)]
        pltpu.make_async_copy(landed, landed, recv_sem.at[from_group]).wait()
        first = inbox[0, pl.ds(from_group * LAYERS, LAYERS)].reshape(rows, half)
        second = inbox[1, pl.ds(from_group * LAYERS, LAYERS)].reshape(rows, half)
        top = jnp.concatenate([first[:, : half // 2], second[:, : half // 2]], axis=1)
        bottom = jnp.concatenate([first[:, half // 2 :], second[:, half // 2 :]], axis=1)
        ordered = jnp.dot(
            permute, jnp.concatenate([top, bottom], axis=0), preferred_element_type=jnp.float32
        ).astype(jnp.bfloat16)
        place = pl.ds(pl.multiple_of(from_group * 32, 32), 32)
        for plane in range(8):
            turned[plane, place, :] = ordered[plane * 32 : plane * 32 + 32]
        return carry

    lax.fori_loop(0, groups, receive_group, 0)
    sent = outbox.at[pl.ds(0, devices - 1)]
    pltpu.make_async_copy(sent, sent, send_sem).wait()


def gram_kernel(planes, out):
    real, imag = planes[0], planes[1]
    size = out.shape[1]
    half = size // 2

    def times(a, b):
        return lax.dot_general(a, b, (((1,), (1,)), ((), ())), preferred_element_type=jnp.float32)

    for i in range(2):
        for j in range(2):
            ri, rj = real[i * half : (i + 1) * half], real[j * half : (j + 1) * half]
            mi, mj = imag[i * half : (i + 1) * half], imag[j * half : (j + 1) * half]
            place = (0, slice(i * half, (i + 1) * half), slice(j * half, (j + 1) * half))
            if i > j:
                out[place] = times(ri, rj) + times(mi, mj)
            elif i < j:
                out[place] = times(mi, rj) - times(ri, mj)
            else:
                row = lax.broadcasted_iota(jnp.int32, (half, half), 0)
                column = lax.broadcasted_iota(jnp.int32, (half, half), 1)
                same = times(ri, rj) + times(mi, mj)
                cross = times(mi, rj) - times(ri, mj)
                out[place] = jnp.where(row >= column, same, cross)


def body(samples, pfb_weights):
    frames = samples[:, 0]
    inputs, count, length = frames.shape
    taps = pfb_weights.shape[0]
    spectra = count - taps + 1
    channels = length // 2
    positions = lax.axis_size("inp")
    groups = positions // LAYERS
    devices = positions * CORES
    rows = 2 * channels // groups
    all_spectra = spectra * CORES
    scale = math.sqrt(2.0 / length) / math.sqrt(all_spectra)
    table = jnp.asarray(dft_table(channels, length, scale).reshape(groups, rows, length))
    per_device = channels // devices
    width = inputs * spectra // 2
    deep = 2 * per_device * 2
    turned = pl.pallas_call(
        turn_kernel,
        out_shape=jax.ShapeDtypeStruct((per_device * 2, inputs * positions, all_spectra), jnp.bfloat16),
        in_specs=[
            pl.BlockSpec(memory_space=pltpu.VMEM),
            pl.BlockSpec(memory_space=pltpu.VMEM),
            pl.BlockSpec(memory_space=pl.ANY),
        ],
        out_specs=pl.BlockSpec(memory_space=pltpu.VMEM),
        scratch_shapes=[
            pltpu.VMEM((count, 128), jnp.float32),
            pltpu.VMEM((inputs * spectra, length), jnp.bfloat16),
            pltpu.VMEM((groups, rows, length), jnp.bfloat16),
            pltpu.VMEM((devices, deep, width), jnp.bfloat16),
            pltpu.VMEM((CORES, positions, deep, width), jnp.bfloat16),
            pltpu.SemaphoreType.DMA((groups,)),
            pltpu.SemaphoreType.DMA,
            pltpu.SemaphoreType.DMA((groups,)),
        ],
        compiler_params=pltpu.CompilerParams(
            collective_id=0, has_side_effects=True, vmem_limit_bytes=VMEM_LIMIT
        ),
    )(frames, pfb_weights, table)
    total = inputs * positions
    return pl.pallas_call(
        gram_kernel,
        grid=(per_device,),
        out_shape=jax.ShapeDtypeStruct((per_device, total, total), jnp.float32),
        in_specs=[pl.BlockSpec((2, total, all_spectra), lambda c: (c, 0, 0))],
        out_specs=pl.BlockSpec((1, total, total), lambda c: (c, 0, 0)),
        compiler_params=pltpu.CompilerParams(vmem_limit_bytes=VMEM_LIMIT),
    )(turned)


def solution(mesh):
    placed = (P("inp", "tm", None, None), P())
    return jax.shard_map(
        body, mesh=mesh, in_specs=placed, out_specs=P(("inp", "tm"), None, None), check_vma=False
    )
```

```python
import functools
import math
import jax
import jax.numpy as jnp
import ml_dtypes
import numpy as np
from jax import lax
from jax.experimental import pallas as pl
from jax.experimental.pallas import tpu as pltpu
from jax.sharding import PartitionSpec as P

MESH = pl.DeviceIdType.MESH
VMEM_LIMIT = 48 * 1024 * 1024
LAYERS = 8
CORES = 2


def dft_table(channels, length, scale):
    phase = np.arange(channels)[:, None] * np.arange(length)[None, :] % length
    angle = np.arange(length) * (2.0 * math.pi / length)
    rows = np.stack([np.cos(angle)[phase], -np.sin(angle)[phase]], axis=1) * scale
    return rows.reshape(channels * 2, length).astype(ml_dtypes.bfloat16)


def turn_kernel(
    samples_hbm, weights_hbm, table, turned, samples, weights, frames, filtered, coeffs, outbox, inbox, sample_sem,
    weight_sem, table_sem, send_sem, recv_sem, ring_sem
):
    position, core = lax.axis_index("inp"), lax.axis_index("tm")
    group, layer = position // LAYERS, lax.rem(position, LAYERS)
    groups, rows, length = coeffs.shape
    count, inputs, _ = samples.shape
    spectra = filtered.shape[0] // inputs
    taps = weights.shape[0]
    peers = LAYERS * CORES

    def fetch(step):
        chunk = lax.rem(group + step, groups)
        return pltpu.make_async_copy(table.at[chunk], coeffs.at[step], table_sem.at[step])

    def start_fetch(step, carry):
        fetch(step).start()
        return carry

    incoming = pltpu.make_async_copy(samples_hbm, samples, sample_sem)
    incoming_weights = pltpu.make_async_copy(weights_hbm, weights, weight_sem)
    incoming_weights.start()
    incoming.start()

    def greet_peers(sem):
        for step in range(1, peers):
            other = lax.rem(layer * CORES + core + step, peers)
            pl.semaphore_signal(
                sem, inc=1, device_id=(group * LAYERS + other // CORES, lax.rem(other, CORES)), device_id_type=MESH
            )

    def greet_groups(sem):
        for step in range(1, groups):
            other = lax.rem(group + step, groups)
            pl.semaphore_signal(sem, inc=1, device_id=(other * LAYERS + layer, core), device_id_type=MESH)

    barrier = pltpu.get_barrier_semaphore()
    greet_peers(barrier)
    greet_groups(barrier)

    lax.fori_loop(0, groups, start_fetch, 0)

    incoming_weights.wait()
    incoming.wait()
    def columns(j, carry):
        cols = pl.ds(pl.multiple_of(j * 128, 128), 128)
        for s in range(count):
            frames[s // 2, s % 2 * inputs : (s % 2 + 1) * inputs, :] = samples[s, :, cols].astype(jnp.float32)
        flat = frames.reshape(frames.shape[0] * 2 * inputs, 128)
        for a in range(inputs):
            total = weights[0:1, cols] * flat[pl.ds(a, spectra, stride=inputs), :]
            for tap in range(1, taps):
                total = total + weights[tap : tap + 1, cols] * flat[pl.ds(a + tap * inputs, spectra, stride=inputs), :]
            filtered[a * spectra : (a + 1) * spectra, cols] = total.astype(jnp.bfloat16)
        return carry

    lax.fori_loop(0, length // 128, columns, 0)

    pl.semaphore_wait(barrier, peers + groups - 2)
    greet_groups(ring_sem)

    half = filtered.shape[0] // 2

    def send_group(step, carry):
        fetch(step).wait()
        found = lax.dot_general(
            coeffs[step], filtered[...], (((1,), (1,)), ((), ())), preferred_element_type=jnp.float32
        )
        found = found.reshape(peers, rows // peers, 2 * half)
        message = jnp.concatenate([found[:, :, :half], found[:, :, half:]], axis=1)
        outbox[pl.ds(step * peers, peers)] = message.astype(jnp.bfloat16)
        to_group = lax.rem(group + step, groups)
        for turn in (4, 3, 5, 2, 6, 1, 7, 0):
            for flip in (0, 1):
                to_layer = lax.rem(layer + turn, LAYERS)
                to_core = lax.rem(core + flip, CORES)
                source = outbox.at[step * peers + to_layer * CORES + to_core]

                def remote():
                    pltpu.make_async_remote_copy(
                        src_ref=source,
                        dst_ref=inbox.at[core, position],
                        send_sem=send_sem,
                        recv_sem=recv_sem.at[group],
                        device_id=(to_group * LAYERS + to_layer, to_core),
                        device_id_type=MESH,
                    ).start()

                if turn == 0 and flip == 0:
                    pl.when(step > 0)(remote)

                    @pl.when(step == 0)
                    def _():
                        pltpu.make_async_copy(source, inbox.at[core, position], recv_sem.at[group]).start()
                else:
                    remote()
        return carry

    send_group(0, 0)
    pl.semaphore_wait(ring_sem, groups - 1)
    lax.fori_loop(1, groups, send_group, 0)

    size = rows * 2
    out_row = lax.broadcasted_iota(jnp.int32, (size, size), 0)
    in_row = lax.broadcasted_iota(jnp.int32, (size, size), 1)
    wanted = (
        (out_row % 2) * (size // 2)
        + (out_row // 4 % LAYERS) * 16
        + (out_row // 2 % 2) * 8
        + (out_row // 64) * 2
        + (out_row // 32 % 2)
    )
    permute = jnp.where(in_row == wanted, 1.0, 0.0).astype(jnp.bfloat16)

    def receive_group(step, carry):
        from_group = lax.rem(group + groups - step, groups)
        landed = inbox.at[:, pl.ds(from_group * LAYERS, LAYERS)]
        pltpu.make_async_copy(landed, landed, recv_sem.at[from_group]).wait()
        first = inbox[0, pl.ds(from_group * LAYERS, LAYERS)].reshape(rows, half)
        second = inbox[1, pl.ds(from_group * LAYERS, LAYERS)].reshape(rows, half)
        top = jnp.concatenate([first[:, : half // 2], second[:, : half // 2]], axis=1)
        bottom = jnp.concatenate([first[:, half // 2 :], second[:, half // 2 :]], axis=1)
        ordered = jnp.dot(
            permute, jnp.concatenate([top, bottom], axis=0), preferred_element_type=jnp.float32
        ).astype(jnp.bfloat16)
        place = pl.ds(pl.multiple_of(from_group * 32, 32), 32)
        for plane in range(8):
            turned[plane, place, :] = ordered[plane * 32 : plane * 32 + 32]
        return carry

    lax.fori_loop(0, groups, receive_group, 0)
    sent = outbox.at[pl.ds(0, groups * peers - 1)]
    pltpu.make_async_copy(sent, sent, send_sem).wait()


def gram_kernel(planes, out, result, out_sem):
    channels, size, _ = result.shape
    half = size // 2
    row = lax.broadcasted_iota(jnp.int32, (half, half), 0)
    column = lax.broadcasted_iota(jnp.int32, (half, half), 1)
    lower = row >= column

    def times(a, b):
        return lax.dot_general(a, b, (((1,), (1,)), ((), ())), preferred_element_type=jnp.float32)

    def deliver(c):
        return pltpu.make_async_copy(result.at[c], out.at[c], out_sem.at[c])

    for c in range(channels):
        real, imag = planes[2 * c], planes[2 * c + 1]
        both = jnp.concatenate([real, imag], axis=1)
        turned = jnp.concatenate([imag, -real], axis=1)
        left = times(jnp.concatenate([both, turned[:half]], axis=0), both[:half])
        right = times(jnp.concatenate([turned, both[half:]], axis=0), both[half:])
        result[c, :half, :half] = jnp.where(lower, left[:half], left[size:])
        result[c, half:, :half] = left[half:size]
        result[c, :half, half:] = right[:half]
        result[c, half:, half:] = jnp.where(lower, right[size:], right[half:size])
        deliver(c).start()
    for c in range(channels):
        deliver(c).wait()


def body(samples, pfb_weights):
    frames = jnp.transpose(samples[:, 0], (1, 0, 2))
    count, inputs, length = frames.shape
    taps = pfb_weights.shape[0]
    spectra = count - taps + 1
    channels = length // 2
    positions = lax.axis_size("inp")
    groups = positions // LAYERS
    devices = positions * CORES
    rows = 2 * channels // groups
    all_spectra = spectra * CORES
    scale = math.sqrt(2.0 / length) / math.sqrt(all_spectra)
    table = jnp.asarray(dft_table(channels, length, scale).reshape(groups, rows, length))
    per_device = channels // devices
    width = inputs * spectra // 2
    deep = 2 * per_device * 2
    turned = pl.pallas_call(
        turn_kernel,
        out_shape=jax.ShapeDtypeStruct((per_device * 2, inputs * positions, all_spectra), jnp.bfloat16),
        in_specs=[
            pl.BlockSpec(memory_space=pltpu.HBM),
            pl.BlockSpec(memory_space=pltpu.HBM),
            pl.BlockSpec(memory_space=pltpu.HBM),
        ],
        out_specs=pl.BlockSpec(memory_space=pltpu.VMEM),
        scratch_shapes=[
            pltpu.VMEM((count, inputs, length), jnp.bfloat16),
            pltpu.VMEM((taps, length), jnp.float32),
            pltpu.VMEM(((count + 1) // 2, 2 * inputs, 128), jnp.float32),
            pltpu.VMEM((inputs * spectra, length), jnp.bfloat16),
            pltpu.VMEM((groups, rows, length), jnp.bfloat16),
            pltpu.VMEM((devices, deep, width), jnp.bfloat16),
            pltpu.VMEM((CORES, positions, deep, width), jnp.bfloat16),
            pltpu.SemaphoreType.DMA,
            pltpu.SemaphoreType.DMA,
            pltpu.SemaphoreType.DMA((groups,)),
            pltpu.SemaphoreType.DMA,
            pltpu.SemaphoreType.DMA((groups,)),
            pltpu.SemaphoreType.REGULAR,
        ],
        compiler_params=pltpu.CompilerParams(
            collective_id=0, has_side_effects=True, vmem_limit_bytes=VMEM_LIMIT
        ),
    )(*(pltpu.with_memory_space_constraint(x, pltpu.HBM) for x in (frames, pfb_weights, table)))
    total = inputs * positions
    return pl.pallas_call(
        gram_kernel,
        out_shape=jax.ShapeDtypeStruct((per_device, total, total), jnp.float32),
        in_specs=[pl.BlockSpec(memory_space=pltpu.VMEM)],
        out_specs=pl.BlockSpec(memory_space=pl.ANY),
        scratch_shapes=[
            pltpu.VMEM((per_device, total, total), jnp.float32),
            pltpu.SemaphoreType.DMA((per_device,)),
        ],
        compiler_params=pltpu.CompilerParams(vmem_limit_bytes=VMEM_LIMIT),
    )(turned)


def solution(mesh):
    placed = (P("inp", "tm", None, None), P())
    return jax.shard_map(
        body, mesh=mesh, in_specs=placed, out_specs=P(("inp", "tm"), None, None), check_vma=False
    )
```

```python
import functools
import math
import jax
import jax.numpy as jnp
import ml_dtypes
import numpy as np
from jax import lax
from jax.experimental import pallas as pl
from jax.experimental.pallas import tpu as pltpu
from jax.sharding import PartitionSpec as P

MESH = pl.DeviceIdType.MESH
VMEM_LIMIT = 48 * 1024 * 1024
LAYERS = 8
CORES = 2
ORDER = (4, 5, 3, 6, 2, 7, 1, 0)


def dft_table(channels, length, scale):
    phase = np.arange(channels)[:, None] * np.arange(length)[None, :] % length
    angle = np.arange(length) * (2.0 * math.pi / length)
    rows = np.stack([np.cos(angle)[phase], -np.sin(angle)[phase]], axis=1) * scale
    return rows.reshape(channels * 2, length).astype(ml_dtypes.bfloat16)


def turn_kernel(
    samples_hbm, weights_hbm, table, turned, samples, weights, frames, filtered, coeffs, outbox, inbox, first_sum, sample_sem,
    weight_sem, table_sem, send_sem, recv_sem, ring_sem
):
    position, core = lax.axis_index("inp"), lax.axis_index("tm")
    group, layer = position // LAYERS, lax.rem(position, LAYERS)
    groups, rows, length = coeffs.shape
    count, inputs, _ = samples.shape
    spectra = filtered.shape[0] // inputs
    taps = weights.shape[0]
    peers = LAYERS * CORES

    def fetch(step):
        chunk = lax.rem(group + step, groups)
        return pltpu.make_async_copy(table.at[chunk], coeffs.at[step], table_sem.at[step])

    def start_fetch(step, carry):
        fetch(step).start()
        return carry

    pieces = sample_sem.shape[0]
    piece = length // pieces
    wide = 256

    def incoming(k):
        cols = pl.ds(k * piece, piece)
        return pltpu.make_async_copy(samples_hbm.at[:, :, cols], samples.at[:, :, cols], sample_sem.at[k])

    incoming_weights = pltpu.make_async_copy(weights_hbm, weights, weight_sem)
    incoming_weights.start()
    for k in range(pieces):
        incoming(k).start()
    fetch(0).start()

    def greet_peers(sem):
        for step in range(1, peers):
            other = lax.rem(layer * CORES + core + step, peers)
            pl.semaphore_signal(
                sem, inc=1, device_id=(group * LAYERS + other // CORES, lax.rem(other, CORES)), device_id_type=MESH
            )

    def greet_group(sem, step):
        other = lax.rem(group + step, groups)
        pl.semaphore_signal(sem, inc=1, device_id=(other * LAYERS + layer, core), device_id_type=MESH)

    def greet_groups(sem):
        for step in range(1, groups):
            greet_group(sem, step)

    barrier = pltpu.get_barrier_semaphore()
    greet_groups(barrier)
    greet_peers(barrier)

    def times(a, b):
        return lax.dot_general(a, b, (((1,), (1,)), ((), ())), preferred_element_type=jnp.float32)

    def combine(j):
        for part in range(wide // 128):
            cols = pl.ds(pl.multiple_of(j * wide + part * 128, 128), 128)
            for s in range(count):
                frames[part, s // 2, s % 2 * inputs : (s % 2 + 1) * inputs, :] = samples[s, :, cols].astype(jnp.float32)
            flat = frames.at[part].reshape(frames.shape[1] * 2 * inputs, 128)
            for a in range(inputs):
                total = weights[0:1, cols] * flat[pl.ds(a, spectra, stride=inputs), :]
                for tap in range(1, taps):
                    total = total + weights[tap : tap + 1, cols] * flat[pl.ds(a + tap * inputs, spectra, stride=inputs), :]
                filtered[a * spectra : (a + 1) * spectra, cols] = total.astype(jnp.bfloat16)

    def partial(j):
        cols = pl.ds(pl.multiple_of(j * wide, wide), wide)
        return times(coeffs[0, :, cols], filtered[:, cols])

    incoming_weights.wait()
    per_piece = piece // wide
    last = length // wide
    signals = 4
    for j in range(last):
        if j % per_piece == 0:
            incoming(j // per_piece).wait()
        if j == last // 2:
            pl.semaphore_wait(barrier, peers + groups - 2)
        if j >= last // 2:
            first_step = 1 + (j - last // 2) * signals
            for step in range(first_step, min(first_step + signals, groups)):
                greet_group(ring_sem, step)
        combine(j)
        if j == 0:
            fetch(0).wait()
            first_sum[...] = partial(0)
        else:
            first_sum[...] += partial(j)
    lax.fori_loop(1, groups, start_fetch, 0)

    half = filtered.shape[0] // 2

    def make_group(step):
        if isinstance(step, int):
            found = first_sum[...]
        else:
            fetch(step).wait()
            found = times(coeffs[step], filtered[...])
        found = found.reshape(peers, rows // peers, 2 * half)
        message = jnp.concatenate([found[:, :, :half], found[:, :, half:]], axis=1)
        outbox[pl.ds(step * peers, peers)] = message.astype(jnp.bfloat16)

    def send(step, to_layer, to_core):
        pltpu.make_async_remote_copy(
            src_ref=outbox.at[step * peers + to_layer * CORES + to_core],
            dst_ref=inbox.at[core, position],
            send_sem=send_sem,
            recv_sem=recv_sem.at[group],
            device_id=(lax.rem(group + step, groups) * LAYERS + to_layer, to_core),
            device_id_type=MESH,
        ).start()

    make_group(0)
    for turn in ORDER:
        for flip in (0, 1):
            if turn or flip:
                send(0, lax.rem(layer + turn, LAYERS), lax.rem(core + flip, CORES))
    pltpu.make_async_copy(outbox.at[layer * CORES + core], inbox.at[core, position], recv_sem.at[group]).start()
    pl.semaphore_wait(ring_sem, groups - 1)

    def send_group(step, carry):
        make_group(step)
        for turn in ORDER:
            for flip in range(CORES):
                send(step, lax.rem(layer + turn, LAYERS), lax.rem(core + flip, CORES))
        return carry

    lax.fori_loop(1, groups, send_group, 0)

    size = rows * 2
    out_row = lax.broadcasted_iota(jnp.int32, (size, size), 0)
    in_row = lax.broadcasted_iota(jnp.int32, (size, size), 1)
    wanted = (
        (out_row % 2) * (size // 2)
        + (out_row // 4 % LAYERS) * 16
        + (out_row // 2 % 2) * 8
        + (out_row // 64) * 2
        + (out_row // 32 % 2)
    )
    permute = jnp.where(in_row == wanted, 1.0, 0.0).astype(jnp.bfloat16)

    def receive_group(step, carry):
        from_group = lax.rem(group + groups - step, groups)
        landed = inbox.at[:, pl.ds(from_group * LAYERS, LAYERS)]
        pltpu.make_async_copy(landed, landed, recv_sem.at[from_group]).wait()
        first = inbox[0, pl.ds(from_group * LAYERS, LAYERS)].reshape(rows, half)
        second = inbox[1, pl.ds(from_group * LAYERS, LAYERS)].reshape(rows, half)
        top = jnp.concatenate([first[:, : half // 2], second[:, : half // 2]], axis=1)
        bottom = jnp.concatenate([first[:, half // 2 :], second[:, half // 2 :]], axis=1)
        ordered = jnp.dot(
            permute, jnp.concatenate([top, bottom], axis=0), preferred_element_type=jnp.float32
        ).astype(jnp.bfloat16)
        place = pl.ds(pl.multiple_of(from_group * 32, 32), 32)
        for plane in range(8):
            turned[plane, place, :] = ordered[plane * 32 : plane * 32 + 32]
        return carry

    lax.fori_loop(0, groups, receive_group, 0)
    sent = outbox.at[pl.ds(0, groups * peers - 1)]
    pltpu.make_async_copy(sent, sent, send_sem).wait()


def gram_kernel(planes, out, result, out_sem):
    channels, size, _ = result.shape
    half = size // 2
    row = lax.broadcasted_iota(jnp.int32, (half, half), 0)
    column = lax.broadcasted_iota(jnp.int32, (half, half), 1)
    lower = row >= column

    def times(a, b):
        return lax.dot_general(a, b, (((1,), (1,)), ((), ())), preferred_element_type=jnp.float32)

    def deliver(c):
        return pltpu.make_async_copy(result.at[c], out.at[c], out_sem.at[c])

    for c in range(channels):
        real, imag = planes[2 * c], planes[2 * c + 1]
        both = jnp.concatenate([real, imag], axis=1)
        turned = jnp.concatenate([imag, -real], axis=1)
        left = times(jnp.concatenate([both, turned[:half]], axis=0), both[:half])
        right = times(jnp.concatenate([turned, both[half:]], axis=0), both[half:])
        result[c, :half, :half] = jnp.where(lower, left[:half], left[size:])
        result[c, half:, :half] = left[half:size]
        result[c, :half, half:] = right[:half]
        result[c, half:, half:] = jnp.where(lower, right[size:], right[half:size])
        deliver(c).start()
    for c in range(channels):
        deliver(c).wait()


def body(samples, pfb_weights):
    frames = jnp.transpose(samples[:, 0], (1, 0, 2))
    count, inputs, length = frames.shape
    taps = pfb_weights.shape[0]
    spectra = count - taps + 1
    channels = length // 2
    positions = lax.axis_size("inp")
    groups = positions // LAYERS
    devices = positions * CORES
    rows = 2 * channels // groups
    all_spectra = spectra * CORES
    scale = math.sqrt(2.0 / length) / math.sqrt(all_spectra)
    table = jnp.asarray(dft_table(channels, length, scale).reshape(groups, rows, length))
    per_device = channels // devices
    width = inputs * spectra // 2
    deep = 2 * per_device * 2
    turned = pl.pallas_call(
        turn_kernel,
        out_shape=jax.ShapeDtypeStruct((per_device * 2, inputs * positions, all_spectra), jnp.bfloat16),
        in_specs=[
            pl.BlockSpec(memory_space=pltpu.HBM),
            pl.BlockSpec(memory_space=pltpu.HBM),
            pl.BlockSpec(memory_space=pltpu.HBM),
        ],
        out_specs=pl.BlockSpec(memory_space=pltpu.VMEM),
        scratch_shapes=[
            pltpu.VMEM((count, inputs, length), jnp.bfloat16),
            pltpu.VMEM((taps, length), jnp.float32),
            pltpu.VMEM((2, (count + 1) // 2, 2 * inputs, 128), jnp.float32),
            pltpu.VMEM((inputs * spectra, length), jnp.bfloat16),
            pltpu.VMEM((groups, rows, length), jnp.bfloat16),
            pltpu.VMEM((devices, deep, width), jnp.bfloat16),
            pltpu.VMEM((CORES, positions, deep, width), jnp.bfloat16),
            pltpu.VMEM((rows, inputs * spectra), jnp.float32),
            pltpu.SemaphoreType.DMA((4,)),
            pltpu.SemaphoreType.DMA,
            pltpu.SemaphoreType.DMA((groups,)),
            pltpu.SemaphoreType.DMA,
            pltpu.SemaphoreType.DMA((groups,)),
            pltpu.SemaphoreType.REGULAR,
        ],
        compiler_params=pltpu.CompilerParams(
            collective_id=0, has_side_effects=True, vmem_limit_bytes=VMEM_LIMIT
        ),
    )(*(pltpu.with_memory_space_constraint(x, pltpu.HBM) for x in (frames, pfb_weights, table)))
    total = inputs * positions
    return pl.pallas_call(
        gram_kernel,
        out_shape=jax.ShapeDtypeStruct((per_device, total, total), jnp.float32),
        in_specs=[pl.BlockSpec(memory_space=pltpu.VMEM)],
        out_specs=pl.BlockSpec(memory_space=pl.ANY),
        scratch_shapes=[
            pltpu.VMEM((per_device, total, total), jnp.float32),
            pltpu.SemaphoreType.DMA((per_device,)),
        ],
        compiler_params=pltpu.CompilerParams(vmem_limit_bytes=VMEM_LIMIT),
    )(turned)


def solution(mesh):
    placed = (P("inp", "tm", None, None), P())
    return jax.shard_map(
        body, mesh=mesh, in_specs=placed, out_specs=P(("inp", "tm"), None, None), check_vma=False
    )
```

```python
import functools
import math
import jax
import jax.numpy as jnp
import ml_dtypes
import numpy as np
from jax import lax
from jax.experimental import pallas as pl
from jax.experimental.pallas import tpu as pltpu
from jax.sharding import PartitionSpec as P

MESH = pl.DeviceIdType.MESH
VMEM_LIMIT = 48 * 1024 * 1024
LAYERS = 8
CORES = 2
PASSES = 2
ORDER = (4, 5, 3, 6, 2, 7, 1, 0)


def dft_table(channels, length, scale):
    phase = np.arange(channels)[:, None] * np.arange(length)[None, :] % length
    angle = np.arange(length) * (2.0 * math.pi / length)
    rows = np.stack([np.cos(angle)[phase], -np.sin(angle)[phase]], axis=1) * scale
    return rows.reshape(channels * 2, length).astype(ml_dtypes.bfloat16)


def turn_kernel(
    samples_hbm, weights_hbm, table, done, late, early, samples, weights, frames, filtered, coeffs, outbox, inbox, first_sum, sample_sem,
    weight_sem, table_sem, send_sem, recv_sem, ring_sem
):
    position, core = lax.axis_index("inp"), lax.axis_index("tm")
    group, layer = position // LAYERS, lax.rem(position, LAYERS)
    groups, rows, length = coeffs.shape
    count, inputs, _ = samples.shape
    spectra = filtered.shape[0] // inputs
    taps = weights.shape[0]
    peers = LAYERS * CORES

    def fetch(step):
        chunk = lax.rem(group + step, groups)
        return pltpu.make_async_copy(table.at[chunk], coeffs.at[step], table_sem.at[step])

    def start_fetch(step, carry):
        fetch(step).start()
        return carry

    pieces = sample_sem.shape[0]
    piece = length // pieces
    wide = 256

    def incoming(k):
        cols = pl.ds(k * piece, piece)
        return pltpu.make_async_copy(samples_hbm.at[:, :, cols], samples.at[:, :, cols], sample_sem.at[k])

    incoming_weights = pltpu.make_async_copy(weights_hbm, weights, weight_sem)
    incoming_weights.start()
    for k in range(pieces):
        incoming(k).start()
    fetch(0).start()

    def greet_peers(sem):
        for step in range(1, peers):
            other = lax.rem(layer * CORES + core + step, peers)
            pl.semaphore_signal(
                sem, inc=1, device_id=(group * LAYERS + other // CORES, lax.rem(other, CORES)), device_id_type=MESH
            )

    def greet_group(sem, step):
        other = lax.rem(group + step, groups)
        pl.semaphore_signal(sem, inc=1, device_id=(other * LAYERS + layer, core), device_id_type=MESH)

    def greet_groups(sem):
        for step in range(1, groups):
            greet_group(sem, step)

    barrier = pltpu.get_barrier_semaphore()
    greet_groups(barrier)
    greet_peers(barrier)

    def times(a, b):
        return lax.dot_general(a, b, (((1,), (1,)), ((), ())), preferred_element_type=jnp.float32)

    def combine(j):
        for part in range(wide // 128):
            cols = pl.ds(pl.multiple_of(j * wide + part * 128, 128), 128)
            for s in range(count):
                frames[part, s // 2, s % 2 * inputs : (s % 2 + 1) * inputs, :] = samples[s, :, cols].astype(jnp.float32)
            flat = frames.at[part].reshape(frames.shape[1] * 2 * inputs, 128)
            for a in range(inputs):
                total = weights[0:1, cols] * flat[pl.ds(a, spectra, stride=inputs), :]
                for tap in range(1, taps):
                    total = total + weights[tap : tap + 1, cols] * flat[pl.ds(a + tap * inputs, spectra, stride=inputs), :]
                filtered[a * spectra : (a + 1) * spectra, cols] = total.astype(jnp.bfloat16)

    def partial(j):
        cols = pl.ds(pl.multiple_of(j * wide, wide), wide)
        return times(coeffs[0, :, cols], filtered[:, cols])

    incoming_weights.wait()
    per_piece = piece // wide
    last = length // wide
    signals = 4
    for j in range(last):
        if j % per_piece == 0:
            incoming(j // per_piece).wait()
        if j == last // 2:
            pl.semaphore_wait(barrier, peers + groups - 2)
        if j >= last // 2:
            first_step = 1 + (j - last // 2) * signals
            for step in range(first_step, min(first_step + signals, groups)):
                greet_group(ring_sem, step)
        combine(j)
        if j == 0:
            fetch(0).wait()
            first_sum[...] = partial(0)
        else:
            first_sum[...] += partial(j)
    lax.fori_loop(1, groups, start_fetch, 0)

    per_pass = groups * peers
    deep = outbox.shape[1]

    def make_group(step):
        if isinstance(step, int):
            found = first_sum[...]
        else:
            fetch(step).wait()
            found = times(coeffs[step], filtered[...])
        found = found.reshape(peers, rows // peers, inputs * spectra)
        size = rows // peers // PASSES
        front = lax.broadcasted_iota(jnp.int32, (peers, rows // peers, spectra), 1) < size
        pairs = [[], []]
        for a in range(0, inputs, 2):
            one = found[:, :, a * spectra : (a + 1) * spectra]
            two = found[:, :, (a + 1) * spectra : (a + 2) * spectra]
            pairs[0].append(jnp.where(front, one, pltpu.roll(two, size, 1)))
            pairs[1].append(jnp.where(front, pltpu.roll(one, size, 1), two))
        for turn in range(PASSES):
            message = jnp.concatenate(pairs[turn], axis=1).astype(jnp.bfloat16)
            outbox[pl.ds(turn * per_pass + step * peers, peers)] = message

    def send(turn, step, to_layer, to_core):
        pltpu.make_async_remote_copy(
            src_ref=outbox.at[turn * per_pass + step * peers + to_layer * CORES + to_core],
            dst_ref=inbox.at[turn, core, position],
            send_sem=send_sem,
            recv_sem=recv_sem.at[turn, group],
            device_id=(lax.rem(group + step, groups) * LAYERS + to_layer, to_core),
            device_id_type=MESH,
        ).start()

    def send_ring(turn, step):
        for away in ORDER:
            for flip in range(CORES):
                send(turn, step, lax.rem(layer + away, LAYERS), lax.rem(core + flip, CORES))

    def send_own_ring(turn):
        for away in ORDER:
            for flip in range(CORES):
                if away or flip:
                    send(turn, 0, lax.rem(layer + away, LAYERS), lax.rem(core + flip, CORES))
        own = outbox.at[turn * per_pass + layer * CORES + core]
        pltpu.make_async_copy(own, inbox.at[turn, core, position], recv_sem.at[turn, group]).start()

    make_group(0)
    send_own_ring(0)
    pl.semaphore_wait(ring_sem, groups - 1)

    def first_pass(step, carry):
        make_group(step)
        send_ring(0, step)
        return carry

    def second_pass(step, carry):
        send_ring(1, step)
        return carry

    lax.fori_loop(1, groups, first_pass, 0)
    send_own_ring(1)
    lax.fori_loop(1, groups, second_pass, 0)

    size = LAYERS * deep
    strip = LAYERS * inputs
    planes = size // strip
    out_row = lax.broadcasted_iota(jnp.int32, (size, size), 0)
    in_row = lax.broadcasted_iota(jnp.int32, (size, size), 1)
    permute = jnp.where(in_row == out_row % strip * planes + out_row // strip, 1.0, 0.0).astype(jnp.bfloat16)

    def receive(turn, ordered_planes):
        def receive_group(step, carry):
            from_group = lax.rem(group + groups - step, groups)
            place = pl.ds(from_group * LAYERS, LAYERS)
            landed = inbox.at[turn, :, place]
            pltpu.make_async_copy(landed, landed, recv_sem.at[turn, from_group]).wait()
            both = jnp.concatenate([inbox[turn, t, place].reshape(size, spectra) for t in range(CORES)], axis=1)
            ordered = jnp.dot(permute, both, preferred_element_type=jnp.float32).astype(jnp.bfloat16)
            where = pl.ds(pl.multiple_of(from_group * strip, strip), strip)
            for plane in range(planes):
                ordered_planes[plane, where, :] = ordered[plane * strip : (plane + 1) * strip]
            return carry

        lax.fori_loop(0, groups, receive_group, 0)

    receive(0, early)
    for c in range(done.shape[0]):
        visibilities(early[2 * c], early[2 * c + 1], done, c)
    receive(1, late)
    sent = outbox.at[pl.ds(0, PASSES * (per_pass - 1))]
    pltpu.make_async_copy(sent, sent, send_sem).wait()


def visibilities(real, imag, result, c):
    size = real.shape[0]
    half = size // 2
    row = lax.broadcasted_iota(jnp.int32, (half, half), 0)
    column = lax.broadcasted_iota(jnp.int32, (half, half), 1)
    lower = row >= column

    def times(a, b):
        return lax.dot_general(a, b, (((1,), (1,)), ((), ())), preferred_element_type=jnp.float32)

    both = jnp.concatenate([real, imag], axis=1)
    turned = jnp.concatenate([imag, -real], axis=1)
    left = times(jnp.concatenate([both, turned[:half]], axis=0), both[:half])
    right = times(jnp.concatenate([turned, both[half:]], axis=0), both[half:])
    result[c, :half, :half] = jnp.where(lower, left[:half], left[size:])
    result[c, half:, :half] = left[half:size]
    result[c, :half, half:] = right[:half]
    result[c, half:, half:] = jnp.where(lower, right[size:], right[half:size])


def finish_kernel(done, planes, out, result, out_sem):
    first = done.shape[0]
    copies = [pltpu.make_async_copy(done.at[c], out.at[c], out_sem.at[c]) for c in range(first)]
    for copy in copies:
        copy.start()
    for c in range(result.shape[0]):
        visibilities(planes[2 * c], planes[2 * c + 1], result, c)
        copies.append(pltpu.make_async_copy(result.at[c], out.at[first + c], out_sem.at[first + c]))
        copies[-1].start()
    for copy in copies:
        copy.wait()


def body(samples, pfb_weights):
    frames = jnp.transpose(samples[:, 0], (1, 0, 2))
    count, inputs, length = frames.shape
    taps = pfb_weights.shape[0]
    spectra = count - taps + 1
    channels = length // 2
    positions = lax.axis_size("inp")
    groups = positions // LAYERS
    devices = positions * CORES
    rows = 2 * channels // groups
    all_spectra = spectra * CORES
    scale = math.sqrt(2.0 / length) / math.sqrt(all_spectra)
    table = jnp.asarray(dft_table(channels, length, scale).reshape(groups, rows, length))
    per_device = channels // devices
    total = inputs * positions
    share = per_device // PASSES
    deep = inputs * share * 2
    done, late = pl.pallas_call(
        turn_kernel,
        out_shape=[
            jax.ShapeDtypeStruct((share, total, total), jnp.float32),
            jax.ShapeDtypeStruct((share * 2, total, all_spectra), jnp.bfloat16),
        ],
        in_specs=[pl.BlockSpec(memory_space=pltpu.HBM)] * 3,
        out_specs=[pl.BlockSpec(memory_space=pltpu.VMEM)] * 2,
        scratch_shapes=[
            pltpu.VMEM((share * 2, total, all_spectra), jnp.bfloat16),
            pltpu.VMEM((count, inputs, length), jnp.bfloat16),
            pltpu.VMEM((taps, length), jnp.float32),
            pltpu.VMEM((2, (count + 1) // 2, 2 * inputs, 128), jnp.float32),
            pltpu.VMEM((inputs * spectra, length), jnp.bfloat16),
            pltpu.VMEM((groups, rows, length), jnp.bfloat16),
            pltpu.VMEM((PASSES * devices, deep, spectra), jnp.bfloat16),
            pltpu.VMEM((PASSES, CORES, positions, deep, spectra), jnp.bfloat16),
            pltpu.VMEM((rows, inputs * spectra), jnp.float32),
            pltpu.SemaphoreType.DMA((4,)),
            pltpu.SemaphoreType.DMA,
            pltpu.SemaphoreType.DMA((groups,)),
            pltpu.SemaphoreType.DMA,
            pltpu.SemaphoreType.DMA((PASSES, groups)),
            pltpu.SemaphoreType.REGULAR,
        ],
        compiler_params=pltpu.CompilerParams(
            collective_id=0, has_side_effects=True, vmem_limit_bytes=VMEM_LIMIT
        ),
    )(*(pltpu.with_memory_space_constraint(x, pltpu.HBM) for x in (frames, pfb_weights, table)))
    return pl.pallas_call(
        finish_kernel,
        out_shape=jax.ShapeDtypeStruct((per_device, total, total), jnp.float32),
        in_specs=[pl.BlockSpec(memory_space=pltpu.VMEM)] * 2,
        out_specs=pl.BlockSpec(memory_space=pl.ANY),
        scratch_shapes=[
            pltpu.VMEM((share, total, total), jnp.float32),
            pltpu.SemaphoreType.DMA((per_device,)),
        ],
        compiler_params=pltpu.CompilerParams(vmem_limit_bytes=VMEM_LIMIT),
    )(done, late)


def solution(mesh):
    placed = (P("inp", "tm", None, None), P())
    return jax.shard_map(
        body, mesh=mesh, in_specs=placed, out_specs=P(("inp", "tm"), None, None), check_vma=False
    )
```

```python
import functools
import math
import jax
import jax.numpy as jnp
import ml_dtypes
import numpy as np
from jax import lax
from jax.experimental import pallas as pl
from jax.experimental.pallas import tpu as pltpu
from jax.sharding import PartitionSpec as P

MESH = pl.DeviceIdType.MESH
VMEM_LIMIT = 48 * 1024 * 1024
LAYERS = 8
CORES = 2
ORDER = (4, 5, 3, 6, 2, 7, 1, 0)


def dft_table(channels, length, scale):
    phase = np.arange(channels)[:, None] * np.arange(length)[None, :] % length
    angle = np.arange(length) * (2.0 * math.pi / length)
    rows = np.stack([np.cos(angle)[phase], -np.sin(angle)[phase]], axis=1) * scale
    return rows.reshape(channels * 2, length).astype(ml_dtypes.bfloat16)


def turn_kernel(
    samples_hbm, weights_hbm, table, turned, samples, weights, frames, filtered, coeffs, outbox, inbox, first_sum, sample_sem,
    weight_sem, table_sem, send_sem, recv_sem, ring_sem
):
    position, core = lax.axis_index("inp"), lax.axis_index("tm")
    group, layer = position // LAYERS, lax.rem(position, LAYERS)
    groups, rows, length = coeffs.shape
    count, inputs, _ = samples.shape
    spectra = filtered.shape[0] // inputs
    taps = weights.shape[0]
    peers = LAYERS * CORES

    def fetch(step):
        chunk = lax.rem(group + step, groups)
        return pltpu.make_async_copy(table.at[chunk], coeffs.at[step], table_sem.at[step])

    def start_fetch(step, carry):
        fetch(step).start()
        return carry

    pieces = sample_sem.shape[0]
    piece = length // pieces
    wide = 256

    def incoming(k):
        cols = pl.ds(k * piece, piece)
        return pltpu.make_async_copy(samples_hbm.at[:, :, cols], samples.at[:, :, cols], sample_sem.at[k])

    incoming_weights = pltpu.make_async_copy(weights_hbm, weights, weight_sem)
    incoming_weights.start()
    for k in range(pieces):
        incoming(k).start()
    fetch(0).start()

    def greet_peers(sem):
        for step in range(1, peers):
            other = lax.rem(layer * CORES + core + step, peers)
            pl.semaphore_signal(
                sem, inc=1, device_id=(group * LAYERS + other // CORES, lax.rem(other, CORES)), device_id_type=MESH
            )

    def greet_group(sem, step):
        other = lax.rem(group + step, groups)
        pl.semaphore_signal(sem, inc=1, device_id=(other * LAYERS + layer, core), device_id_type=MESH)

    def greet_groups(sem):
        for step in range(1, groups):
            greet_group(sem, step)

    barrier = pltpu.get_barrier_semaphore()
    greet_groups(barrier)
    greet_peers(barrier)

    def times(a, b):
        return lax.dot_general(a, b, (((1,), (1,)), ((), ())), preferred_element_type=jnp.float32)

    def combine(j):
        for part in range(wide // 128):
            cols = pl.ds(pl.multiple_of(j * wide + part * 128, 128), 128)
            for s in range(count):
                frames[part, s // 2, s % 2 * inputs : (s % 2 + 1) * inputs, :] = samples[s, :, cols].astype(jnp.float32)
            flat = frames.at[part].reshape(frames.shape[1] * 2 * inputs, 128)
            for a in range(inputs):
                total = weights[0:1, cols] * flat[pl.ds(a, spectra, stride=inputs), :]
                for tap in range(1, taps):
                    total = total + weights[tap : tap + 1, cols] * flat[pl.ds(a + tap * inputs, spectra, stride=inputs), :]
                filtered[a * spectra : (a + 1) * spectra, cols] = total.astype(jnp.bfloat16)

    def partial(j):
        cols = pl.ds(pl.multiple_of(j * wide, wide), wide)
        return times(coeffs[0, :, cols], filtered[:, cols])

    incoming_weights.wait()
    per_piece = piece // wide
    last = length // wide
    signals = 4
    for j in range(last):
        if j % per_piece == 0:
            incoming(j // per_piece).wait()
        if j == last // 2:
            pl.semaphore_wait(barrier, peers + groups - 2)
        if j >= last // 2:
            first_step = 1 + (j - last // 2) * signals
            for step in range(first_step, min(first_step + signals, groups)):
                greet_group(ring_sem, step)
        combine(j)
        if j == 0:
            fetch(0).wait()
            first_sum[...] = partial(0)
        else:
            first_sum[...] += partial(j)
    lax.fori_loop(1, groups, start_fetch, 0)

    half = filtered.shape[0] // 2

    def make_group(step):
        if isinstance(step, int):
            found = first_sum[...]
        else:
            fetch(step).wait()
            found = times(coeffs[step], filtered[...])
        found = found.reshape(peers, rows // peers, 2 * half)
        message = jnp.concatenate([found[:, :, :half], found[:, :, half:]], axis=1)
        outbox[pl.ds(step * peers, peers)] = message.astype(jnp.bfloat16)

    def send(step, to_layer, to_core):
        pltpu.make_async_remote_copy(
            src_ref=outbox.at[step * peers + to_layer * CORES + to_core],
            dst_ref=inbox.at[core, position],
            send_sem=send_sem,
            recv_sem=recv_sem.at[group],
            device_id=(lax.rem(group + step, groups) * LAYERS + to_layer, to_core),
            device_id_type=MESH,
        ).start()

    make_group(0)
    for turn in ORDER:
        for flip in (0, 1):
            if turn or flip:
                send(0, lax.rem(layer + turn, LAYERS), lax.rem(core + flip, CORES))
    pltpu.make_async_copy(outbox.at[layer * CORES + core], inbox.at[core, position], recv_sem.at[group]).start()

    def send_group(step, carry):
        make_group(step)

        @pl.when(step == 1)
        def _():
            pl.semaphore_wait(ring_sem, groups - 1)

        for turn in ORDER:
            for flip in range(CORES):
                send(step, lax.rem(layer + turn, LAYERS), lax.rem(core + flip, CORES))
        return carry

    lax.fori_loop(1, groups, send_group, 0)

    size = rows * 2
    out_row = lax.broadcasted_iota(jnp.int32, (size, size), 0)
    in_row = lax.broadcasted_iota(jnp.int32, (size, size), 1)
    wanted = (
        (out_row % 2) * (size // 2)
        + (out_row // 4 % LAYERS) * 16
        + (out_row // 2 % 2) * 8
        + (out_row // 64) * 2
        + (out_row // 32 % 2)
    )
    permute = jnp.where(in_row == wanted, 1.0, 0.0).astype(jnp.bfloat16)

    def receive_group(step, carry):
        from_group = lax.rem(group + groups - step, groups)
        landed = inbox.at[:, pl.ds(from_group * LAYERS, LAYERS)]
        pltpu.make_async_copy(landed, landed, recv_sem.at[from_group]).wait()
        first = inbox[0, pl.ds(from_group * LAYERS, LAYERS)].reshape(rows, half)
        second = inbox[1, pl.ds(from_group * LAYERS, LAYERS)].reshape(rows, half)
        top = jnp.concatenate([first[:, : half // 2], second[:, : half // 2]], axis=1)
        bottom = jnp.concatenate([first[:, half // 2 :], second[:, half // 2 :]], axis=1)
        ordered = jnp.dot(
            permute, jnp.concatenate([top, bottom], axis=0), preferred_element_type=jnp.float32
        ).astype(jnp.bfloat16)
        place = pl.ds(pl.multiple_of(from_group * 32, 32), 32)
        for plane in range(8):
            turned[plane, place, :] = ordered[plane * 32 : plane * 32 + 32]
        return carry

    lax.fori_loop(0, groups, receive_group, 0)
    sent = outbox.at[pl.ds(0, groups * peers - 1)]
    pltpu.make_async_copy(sent, sent, send_sem).wait()


def gram_kernel(planes, out, result, out_sem):
    channels, size, _ = result.shape
    half = size // 2
    row = lax.broadcasted_iota(jnp.int32, (half, half), 0)
    column = lax.broadcasted_iota(jnp.int32, (half, half), 1)
    lower = row >= column

    def times(a, b):
        return lax.dot_general(a, b, (((1,), (1,)), ((), ())), preferred_element_type=jnp.float32)

    def deliver(c):
        return pltpu.make_async_copy(result.at[c], out.at[c], out_sem.at[c])

    for c in range(channels):
        real, imag = planes[2 * c], planes[2 * c + 1]
        both = jnp.concatenate([real, imag], axis=1)
        turned = jnp.concatenate([imag, -real], axis=1)
        left = times(jnp.concatenate([both, turned[:half]], axis=0), both[:half])
        right = times(jnp.concatenate([turned, both[half:]], axis=0), both[half:])
        result[c, :half, :half] = jnp.where(lower, left[:half], left[size:])
        result[c, half:, :half] = left[half:size]
        result[c, :half, half:] = right[:half]
        result[c, half:, half:] = jnp.where(lower, right[size:], right[half:size])
        deliver(c).start()
    for c in range(channels):
        deliver(c).wait()


def body(samples, pfb_weights):
    frames = jnp.transpose(samples[:, 0], (1, 0, 2))
    count, inputs, length = frames.shape
    taps = pfb_weights.shape[0]
    spectra = count - taps + 1
    channels = length // 2
    positions = lax.axis_size("inp")
    groups = positions // LAYERS
    devices = positions * CORES
    rows = 2 * channels // groups
    all_spectra = spectra * CORES
    scale = math.sqrt(2.0 / length) / math.sqrt(all_spectra)
    table = jnp.asarray(dft_table(channels, length, scale).reshape(groups, rows, length))
    per_device = channels // devices
    width = inputs * spectra // 2
    deep = 2 * per_device * 2
    turned = pl.pallas_call(
        turn_kernel,
        out_shape=jax.ShapeDtypeStruct((per_device * 2, inputs * positions, all_spectra), jnp.bfloat16),
        in_specs=[
            pl.BlockSpec(memory_space=pltpu.HBM),
            pl.BlockSpec(memory_space=pltpu.HBM),
            pl.BlockSpec(memory_space=pltpu.HBM),
        ],
        out_specs=pl.BlockSpec(memory_space=pltpu.VMEM),
        scratch_shapes=[
            pltpu.VMEM((count, inputs, length), jnp.bfloat16),
            pltpu.VMEM((taps, length), jnp.float32),
            pltpu.VMEM((2, (count + 1) // 2, 2 * inputs, 128), jnp.float32),
            pltpu.VMEM((inputs * spectra, length), jnp.bfloat16),
            pltpu.VMEM((groups, rows, length), jnp.bfloat16),
            pltpu.VMEM((devices, deep, width), jnp.bfloat16),
            pltpu.VMEM((CORES, positions, deep, width), jnp.bfloat16),
            pltpu.VMEM((rows, inputs * spectra), jnp.float32),
            pltpu.SemaphoreType.DMA((4,)),
            pltpu.SemaphoreType.DMA,
            pltpu.SemaphoreType.DMA((groups,)),
            pltpu.SemaphoreType.DMA,
            pltpu.SemaphoreType.DMA((groups,)),
            pltpu.SemaphoreType.REGULAR,
        ],
        compiler_params=pltpu.CompilerParams(
            collective_id=0, has_side_effects=True, vmem_limit_bytes=VMEM_LIMIT
        ),
    )(*(pltpu.with_memory_space_constraint(x, pltpu.HBM) for x in (frames, pfb_weights, table)))
    total = inputs * positions
    return pl.pallas_call(
        gram_kernel,
        out_shape=jax.ShapeDtypeStruct((per_device, total, total), jnp.float32),
        in_specs=[pl.BlockSpec(memory_space=pltpu.VMEM)],
        out_specs=pl.BlockSpec(memory_space=pl.ANY),
        scratch_shapes=[
            pltpu.VMEM((per_device, total, total), jnp.float32),
            pltpu.SemaphoreType.DMA((per_device,)),
        ],
        compiler_params=pltpu.CompilerParams(vmem_limit_bytes=VMEM_LIMIT),
    )(turned)


def solution(mesh):
    placed = (P("inp", "tm", None, None), P())
    return jax.shard_map(
        body, mesh=mesh, in_specs=placed, out_specs=P(("inp", "tm"), None, None), check_vma=False
    )
```
